32 devices in a mesh: groups: 2 (over x), row: 8 (over z, y), col: 2 (over core).
Axes of the slice: x: 2, y: 2, z: 4, core: 2. Of those that a mesh axis runs over, the one named last changes fastest.
Arguments:
- patches: float32 [8192, 2048], P(('groups', 'row'), 'col'), parts along dimension 0, may hold values from -170 to 170
Outputs:
- rotated: float32 [8192, 2048], P(('groups', 'row'), 'col'), parts along dimension 0
The draws below stay inside these ranges and needn't reach their ends.
There are 2 independent parts, one for each index of `groups`. The reference program is written for one: setup_inputs(seed, part) draws one part's arguments, and reference() takes and returns one part's arrays. A program takes and returns all parts, laid end to end along the dimension named above; each array names one. Nothing has to cross between parts.
All inputs are finite; a program needn't handle non-finite values.
Results may differ from the reference program's by a relative error of at most 0.0003.
Values sent between devices are 32-bit elements; how exact they have to be, the bound alone decides.
A program may use at most 128 MiB of HBM per device.

```python
import jax
import jax.numpy as jnp
import numpy as np
from jax import lax

BW = 128
BLOCKS = 16
ROUNDS = 4
ROWS = 4096
COLS = 2048


def draw_patches(key, part):
    key = jax.random.fold_in(key, 7)
    keys = jax.random.split(key, 5)
    position = jnp.arange(ROWS, dtype=jnp.float32) / ROWS
    row_scale = jnp.exp(jnp.log(3.0) * (position - 0.5) + jax.random.uniform(keys[0], (ROWS,), jnp.float32, -0.7, 0.7))
    col_scale = jnp.exp(jax.random.uniform(keys[1], (COLS,), jnp.float32, -1.2, 1.2))
    common = jax.random.truncated_normal(keys[2], -4.0, 4.0, (ROWS,), jnp.float32)
    noise = jax.random.truncated_normal(keys[3], -4.0, 4.0, (ROWS, COLS), jnp.float32)
    loading = jax.random.uniform(keys[4], (COLS,), jnp.float32, -1.5, 1.5)
    values = row_scale[:, None] * col_scale[None, :] * (noise + loading[None, :] * common[:, None])
    return values.astype(jnp.float32)


def setup_inputs(seed: int = 0, part: int = 0) -> dict:
    key_of = jax.random.split(jax.random.key(seed), 2)
    part_splits = jax.random.split(jax.random.fold_in(key_of[1], part), 2)
    return {
        "patches": draw_patches(jax.random.fold_in(jax.random.fold_in(key_of[1], part), 71), part),
    }


def source_slots(block_total):
    cycle_order = list(range(2, block_total - 1, 2)) + [block_total - 1] + list(range(block_total - 3, 0, -2))
    sources = np.zeros(block_total, dtype=np.int32)
    length = len(cycle_order)
    for place in range(length):
        sources[cycle_order[(place + 1) % length]] = cycle_order[place]
    return sources

def inverse_root(matrix, identity):
    high = lax.Precision.HIGHEST
    current = matrix * 0.5
    other = identity
    for step in range(8):
        middle = 1.5 * identity - 0.5 * jnp.matmul(other, current, precision=high)
        current = jnp.matmul(current, middle, precision=high)
        other = jnp.matmul(middle, other, precision=high)
    return other * 0.7071067811865476

def rotation(gram_left, gram_right, gram_cross):
    high = lax.Precision.HIGHEST
    width_now = gram_left.shape[-1]
    identity = jnp.broadcast_to(jnp.eye(width_now, dtype=jnp.float32), gram_left.shape)
    trace_left = lax.optimization_barrier(jnp.sum(jnp.diagonal(gram_left, axis1=1, axis2=2), axis=-1))
    trace_right = lax.optimization_barrier(jnp.sum(jnp.diagonal(gram_right, axis1=1, axis2=2), axis=-1))
    corr = gram_cross / jnp.sqrt(trace_left * trace_right)[:, None, None]
    corr_t = jnp.swapaxes(corr, 1, 2)
    inverse_one = inverse_root(identity + jnp.matmul(corr, corr_t, precision=high), identity)
    inverse_two = inverse_root(identity + jnp.matmul(corr_t, corr, precision=high), identity)
    upper = jnp.concatenate([inverse_one, -jnp.matmul(corr, inverse_two, precision=high)], axis=2)
    lower_rows = jnp.concatenate([jnp.matmul(corr_t, inverse_one, precision=high), inverse_two], axis=2)
    return jnp.concatenate([upper, lower_rows], axis=1)

def reference(patches):
    high = lax.Precision.HIGHEST
    blocks = patches.reshape(ROWS, BLOCKS, BW)
    sources = source_slots(BLOCKS)
    for round_index in range(ROUNDS):
        paired = blocks.reshape(ROWS, BLOCKS // 2, 2 * BW)
        gram = jnp.einsum('rpi,rpj->pij', paired, paired, precision=high)
        rotations = rotation(gram[:, :BW, :BW], gram[:, BW:, BW:], gram[:, :BW, BW:])
        paired = jnp.einsum('rpi,pij->rpj', paired, rotations, precision=high)
        blocks = paired.reshape(ROWS, BLOCKS, BW)
        if round_index + 1 < ROUNDS:
            blocks = blocks[:, sources, :]
    return blocks.reshape(ROWS, COLS)
```

```python
import functools

import jax
import jax.numpy as jnp
from jax import lax
from jax.experimental import pallas as pl
from jax.experimental.pallas import tpu as pltpu
from jax.sharding import PartitionSpec as P

BW = 128
ROUNDS = 4
STEPS = 8
EXACT = 3
TRACE_ROWS = 8
MESH = pl.DeviceIdType.MESH
F32 = jnp.float32
BF16 = jnp.bfloat16


def split(x):
    high = x.astype(BF16)
    return high, (x - high.astype(F32)).astype(BF16)


def dot(a, b):
    return jnp.dot(a, b, preferred_element_type=F32)


def product(a, b):
    width = b.shape[1]
    right = jnp.concatenate(split(b), axis=1)
    both = dot(jnp.concatenate(split(a), axis=1), jnp.concatenate([right, right], axis=0))
    return both[:, :width] + both[:, width:]


def rough(a, b):
    return dot(a.astype(BF16), b.astype(BF16))


def identity():
    rows = lax.broadcasted_iota(jnp.int32, (BW, BW), 0)
    columns = lax.broadcasted_iota(jnp.int32, (BW, BW), 1)
    return jnp.where(rows == columns, 1.0, 0.0).astype(F32)


def inverse_roots(squares, eye):
    errors = [0.5 * eye - 0.5 * square for square in squares]
    roots = [eye + 0.5 * error for error in errors]
    for step in range(1, STEPS):
        times = product if step < EXACT else rough
        seconds = [times(error, error) for error in errors]
        thirds = [times(second, error) for second, error in zip(seconds, errors)]
        errors = [0.75 * second + 0.25 * third for second, third in zip(seconds, thirds)]
        roots = [root + 0.5 * times(root, error) for root, error in zip(roots, errors)]
    return [root * 0.7071067811865476 for root in roots]


def kernel(n, pairs, per, x_ref, out_ref, buf, part, landed, total, spare,
           in_sem, out_sem, rs_send, rs_recv, ag_send, ag_recv, swap_send, swap_recv):
    me = lax.axis_index("row")
    col = lax.axis_index("col")
    stages = pairs // per
    slots = 2 * pairs
    chunk = per * BW // n
    own = [lax.rem(me + j, n) for j in range(n)]
    sign = jnp.where(col == 0, 1.0, -1.0).astype(F32)

    def columns(slot):
        place = jnp.where(col == 0, slot, slots - 1 - slot)
        return pl.ds(pl.multiple_of(place * BW, BW), BW)

    loads = [
        pltpu.make_async_copy(x_ref.at[:, columns(slot)], buf.at[0, slot], in_sem.at[slot])
        for slot in range(slots)
    ]
    for load in loads:
        load.start()

    barrier = pltpu.get_barrier_semaphore()
    for j in range(1, n):
        pl.semaphore_signal(barrier, inc=1, device_id={"row": own[j]}, device_id_type=MESH)
    pl.semaphore_signal(barrier, inc=1, device_id={"col": 1 - col}, device_id_type=MESH)

    def gram(r, pair):
        stage, at = pair // per, pair % per
        left = buf[r, 2 * pair]
        right = buf[r, 2 * pair + 1]
        left_halves = jnp.concatenate(split(left), axis=1)
        right_halves = jnp.concatenate(split(right), axis=1)
        both = lax.dot_general(
            left_halves, right_halves, (((0,), (0,)), ((), ())), preferred_element_type=F32
        )
        cross = both[:BW, :BW] + both[:BW, BW:] + both[BW:, :BW] + both[BW:, BW:]
        owners = BW // chunk
        for piece in range(owners):
            rows = cross[piece * chunk:(piece + 1) * chunk]
            part[r, stage, at * owners + piece, :chunk, :] = rows
        return [jnp.sum(block * block, axis=0, keepdims=True) for block in (left, right)]

    def send_parts(r, stage, sums):
        missing = TRACE_ROWS - len(sums)
        if missing:
            sums = sums + [jnp.zeros((missing, BW), F32)]
        rows = jnp.concatenate(sums, axis=0)
        for owner in range(n):
            part[r, stage, owner, chunk:, :] = rows
        for j in range(1, n):
            pltpu.make_async_remote_copy(
                src_ref=part.at[r, stage, own[j]],
                dst_ref=landed.at[r, stage, j - 1],
                send_sem=rs_send.at[r, stage],
                recv_sem=rs_recv.at[r, stage],
                device_id={"row": own[j]},
                device_id_type=MESH,
            ).start()

    def send_sums(r, stage):
        everyone = landed.at[r, stage]
        pltpu.make_async_copy(everyone, everyone, rs_recv.at[r, stage]).wait()
        summed = part[r, stage, me]
        for j in range(n - 1):
            summed = summed + landed[r, stage, j]
        mine = total.at[r, stage, pl.ds(pl.multiple_of(me * chunk, 8), chunk)]
        mine[...] = summed[:chunk]
        for j in range(1, n):
            pltpu.make_async_remote_copy(
                src_ref=mine,
                dst_ref=mine,
                send_sem=ag_send.at[r, stage],
                recv_sem=ag_recv.at[r, stage],
                device_id={"row": own[j]},
                device_id_type=MESH,
            ).start()
        return jnp.sum(summed[chunk:], axis=1, keepdims=True)

    def gathered_bytes(r, stage):
        return total.at[r, stage, pl.ds(0, (n - 1) * chunk)]

    def rotations(r, stage, traces, eye):
        held = gathered_bytes(r, stage)
        pltpu.make_async_copy(held, held, ag_recv.at[r, stage]).wait()
        corrs = []
        for at in range(per):
            size = jnp.sqrt(traces[2 * at:2 * at + 1] * traces[2 * at + 1:2 * at + 2])
            corrs.append(total[r, stage, at * BW:(at + 1) * BW, :] / size)
        turned = [corr.T for corr in corrs]
        squares = []
        for corr, corr_t in zip(corrs, turned):
            squares += [product(corr, corr_t), product(corr_t, corr)]
        roots = inverse_roots(squares, eye)
        results = []
        for at in range(per):
            one, two = roots[2 * at], roots[2 * at + 1]
            upper = jnp.concatenate([one, -sign * product(corrs[at], two)], axis=1)
            lower = jnp.concatenate([sign * product(turned[at], one), two], axis=1)
            results.append(jnp.concatenate([upper, lower], axis=0))
        return results

    def apply(r, pair, rotation):
        block = jnp.concatenate([buf[r, 2 * pair], buf[r, 2 * pair + 1]], axis=1)
        high, low = split(block)
        turn_high, turn_low = split(rotation)
        return dot(high, turn_high) + dot(low, turn_high) + dot(high, turn_low)

    def swap(r):
        return pltpu.make_async_remote_copy(
            src_ref=spare.at[r],
            dst_ref=buf.at[r + 1, slots - 1],
            send_sem=swap_send.at[r],
            recv_sem=swap_recv.at[r],
            device_id={"col": 1 - col},
            device_id_type=MESH,
        )

    def place(r, pair, result):
        first, second = result[:, :BW], result[:, BW:]
        if pair == pairs - 1:
            spare[r] = first
            swap(r).start()
        else:
            buf[r + 1, 2 * pair + 2 if pair else 0] = first
        buf[r + 1, 2 * pair - 1 if pair else 2] = second

    def turn_slots(rotation):
        swapped = jnp.concatenate([rotation[:, BW:], rotation[:, :BW]], axis=1)
        return jnp.where(col == 0, rotation, swapped)

    def sums_round(r, first):
        all_sums = []
        for stage in range(stages):
            sums = []
            for at in range(per):
                pair = stage * per + at
                if first:
                    loads[2 * pair].wait()
                    loads[2 * pair + 1].wait()
                sums += gram(r, pair)
            if first and stage == 0:
                pl.semaphore_wait(barrier, n)
            send_parts(r, stage, sums)
        return [send_sums(r, stage) for stage in range(stages)]

    def rotate_round(r, traces, last):
        eye = identity()
        for stage in reversed(range(stages)):
            turns = rotations(r, stage, traces[stage], eye)
            for at in reversed(range(per)):
                pair = stage * per + at
                turn = turns[at]
                if last:
                    result = apply(r, pair, turn)
                    for side in range(2):
                        buf[r + 1, 2 * pair + side] = result[:, side * BW:(side + 1) * BW]
                        store(2 * pair + side).start()
                else:
                    if pair == 0:
                        turn = turn_slots(turn)
                    place(r, pair, apply(r, pair, turn))

    def store(slot):
        return pltpu.make_async_copy(
            buf.at[ROUNDS, slot], out_ref.at[:, columns(slot)], out_sem.at[slot]
        )

    for r in range(ROUNDS):
        traces = sums_round(r, r == 0)
        rotate_round(r, traces, r == ROUNDS - 1)
        if r < ROUNDS - 1:
            swap(r).wait_recv()

    for slot in range(slots):
        store(slot).wait()
    for r in range(ROUNDS):
        if r < ROUNDS - 1:
            swap(r).wait_send()
        for stage in range(stages):
            everyone = landed.at[r, stage]
            pltpu.make_async_copy(everyone, everyone, rs_send.at[r, stage]).wait()
            held = gathered_bytes(r, stage)
            pltpu.make_async_copy(held, held, ag_send.at[r, stage]).wait()


def shards(n, patches):
    rows, width = patches.shape
    pairs = width // (2 * BW)
    per = max(2, min(pairs, 8 * n // BW))
    stages = pairs // per
    chunk = per * BW // n
    message = chunk + TRACE_ROWS
    return pl.pallas_call(
        functools.partial(kernel, n, pairs, per),
        out_shape=jax.ShapeDtypeStruct((rows, width), F32),
        in_specs=[pl.BlockSpec(memory_space=pl.ANY)],
        out_specs=pl.BlockSpec(memory_space=pl.ANY),
        scratch_shapes=[
            pltpu.VMEM((ROUNDS + 1, 2 * pairs, rows, BW), F32),
            pltpu.VMEM((ROUNDS, stages, n, message, BW), F32),
            pltpu.VMEM((ROUNDS, stages, n - 1, message, BW), F32),
            pltpu.VMEM((ROUNDS, stages, per * BW, BW), F32),
            pltpu.VMEM((ROUNDS - 1, rows, BW), F32),
            pltpu.SemaphoreType.DMA((2 * pairs,)),
            pltpu.SemaphoreType.DMA((2 * pairs,)),
            pltpu.SemaphoreType.DMA((ROUNDS, stages)),
            pltpu.SemaphoreType.DMA((ROUNDS, stages)),
            pltpu.SemaphoreType.DMA((ROUNDS, stages)),
            pltpu.SemaphoreType.DMA((ROUNDS, stages)),
            pltpu.SemaphoreType.DMA((ROUNDS - 1,)),
            pltpu.SemaphoreType.DMA((ROUNDS - 1,)),
        ],
        compiler_params=pltpu.CompilerParams(
            collective_id=0, has_side_effects=True, vmem_limit_bytes=48 * 1024 * 1024
        ),
    )(patches)


def solution(mesh):
    placed = P(("groups", "row"), "col")
    return jax.shard_map(
        functools.partial(shards, mesh.shape["row"]),
        mesh=mesh,
        in_specs=(placed,),
        out_specs=placed,
        check_vma=False,
    )
```

```python
import functools

import jax
import jax.numpy as jnp
from jax import lax
from jax.experimental import pallas as pl
from jax.experimental.pallas import tpu as pltpu
from jax.sharding import PartitionSpec as P

BW = 128
ROUNDS = 4
STEPS = 8
EXACT = 3
MESH = pl.DeviceIdType.MESH
F32 = jnp.float32
BF16 = jnp.bfloat16


def split(x):
    high = x.astype(BF16)
    return high, (x - high.astype(F32)).astype(BF16)


def dot(a, b):
    return jnp.dot(a, b, preferred_element_type=F32)


def product(a, b):
    width = b.shape[1]
    right = jnp.concatenate(split(b), axis=1)
    both = dot(jnp.concatenate(split(a), axis=1), jnp.concatenate([right, right], axis=0))
    return both[:, :width] + both[:, width:]


def rough(a, b):
    return dot(a.astype(BF16), b.astype(BF16))


def identity():
    rows = lax.broadcasted_iota(jnp.int32, (BW, BW), 0)
    columns = lax.broadcasted_iota(jnp.int32, (BW, BW), 1)
    return jnp.where(rows == columns, 1.0, 0.0).astype(F32)


def inverse_roots(squares, eye):
    errors = [0.5 * eye - 0.5 * square for square in squares]
    roots = [eye + 0.5 * error for error in errors]
    for step in range(1, STEPS):
        times = product if step < EXACT else rough
        if step <= EXACT:
            seconds = [times(error, error) for error in errors]
        else:
            both = [rough(error, jnp.concatenate([error, root], axis=1))
                    for error, root in zip(errors, roots)]
            seconds = [two[:, :BW] for two in both]
            roots = [root + 0.5 * two[:, BW:] for root, two in zip(roots, both)]
        thirds = [times(second, error) for second, error in zip(seconds, errors)]
        errors = [0.75 * second + 0.25 * third for second, third in zip(seconds, thirds)]
        if step < EXACT:
            roots = [root + 0.5 * times(root, error) for root, error in zip(roots, errors)]
    roots = [root + 0.5 * rough(error, root) for root, error in zip(roots, errors)]
    return [root * 0.7071067811865476 for root in roots]


def kernel(n, pairs, per, x_ref, out_ref, buf, part, landed, total, spare, norms,
           in_sem, out_sem, norm_send, norm_recv, rs_send, rs_recv, ag_send, ag_recv, swap_send, swap_recv):
    me = lax.axis_index("row")
    col = lax.axis_index("col")
    stages = pairs // per
    slots = 2 * pairs
    chunk = per * BW // n
    own = [lax.rem(me + j, n) for j in range(n)]
    order = sorted(range(1, n), key=lambda j: abs(2 * j - n))
    sign = jnp.where(col == 0, 1.0, -1.0).astype(F32)

    def columns(slot):
        place = jnp.where(col == 0, slot, slots - 1 - slot)
        return pl.ds(pl.multiple_of(place * BW, BW), BW)

    loads = [
        pltpu.make_async_copy(x_ref.at[:, columns(slot)], buf.at[0, slot], in_sem.at[slot])
        for slot in range(slots)
    ]
    for load in reversed(loads):
        load.start()

    barrier = pltpu.get_barrier_semaphore()
    for j in range(1, n):
        pl.semaphore_signal(barrier, inc=1, device_id={"row": own[j]}, device_id_type=MESH)
    pl.semaphore_signal(barrier, inc=1, device_id={"col": 1 - col}, device_id_type=MESH)

    def gram(r, pair):
        stage, at = pair // per, pair % per
        left_halves = jnp.concatenate(split(buf[r, 2 * pair]), axis=1)
        right_halves = jnp.concatenate(split(buf[r, 2 * pair + 1]), axis=1)
        both = lax.dot_general(
            left_halves, right_halves, (((0,), (0,)), ((), ())), preferred_element_type=F32
        )
        cross = both[:BW, :BW] + both[:BW, BW:] + both[BW:, :BW] + both[BW:, BW:]
        part[r, stage, at * BW:(at + 1) * BW, :] = cross

    def send_traces(r):
        blocks = [buf[r, slot] for slot in range(slots)]
        sums = [jnp.sum(block * block, axis=0, keepdims=True) for block in blocks]
        norms[r, n - 1] = jnp.concatenate(sums, axis=0)
        for j in order:
            pltpu.make_async_remote_copy(
                src_ref=norms.at[r, n - 1],
                dst_ref=norms.at[r, j - 1],
                send_sem=norm_send.at[r],
                recv_sem=norm_recv.at[r],
                device_id={"row": own[j]},
                device_id_type=MESH,
            ).start()

    def traces_of(r):
        held = norms.at[r, pl.ds(0, n - 1)]
        pltpu.make_async_copy(held, held, norm_recv.at[r]).wait()
        summed = norms[r, 0]
        for j in range(1, n):
            summed = summed + norms[r, j]
        return jnp.sum(summed, axis=1, keepdims=True)

    def send_parts(r, stage):
        for j in order:
            rows = pl.ds(pl.multiple_of(own[j] * chunk, 8), chunk)
            pltpu.make_async_remote_copy(
                src_ref=part.at[r, stage, rows],
                dst_ref=landed.at[r, stage, j - 1],
                send_sem=rs_send.at[r, stage],
                recv_sem=rs_recv.at[r, stage],
                device_id={"row": own[j]},
                device_id_type=MESH,
            ).start()

    def send_sums(r, stage):
        everyone = landed.at[r, stage]
        pltpu.make_async_copy(everyone, everyone, rs_recv.at[r, stage]).wait()
        rows = pl.ds(pl.multiple_of(me * chunk, 8), chunk)
        summed = part[r, stage, rows]
        for j in range(n - 1):
            summed = summed + landed[r, stage, j]
        mine = total.at[r, stage, rows]
        mine[...] = summed
        for j in order:
            pltpu.make_async_remote_copy(
                src_ref=mine,
                dst_ref=mine,
                send_sem=ag_send.at[r, stage],
                recv_sem=ag_recv.at[r, stage],
                device_id={"row": own[j]},
                device_id_type=MESH,
            ).start()

    def gathered_bytes(r, stage):
        return total.at[r, stage, pl.ds(0, (n - 1) * chunk)]

    def rotations(r, traces, eye):
        for stage in reversed(range(stages)):
            held = gathered_bytes(r, stage)
            pltpu.make_async_copy(held, held, ag_recv.at[r, stage]).wait()
        corrs = []
        for pair in range(pairs):
            size = jnp.sqrt(traces[2 * pair:2 * pair + 1] * traces[2 * pair + 1:2 * pair + 2])
            stage, at = pair // per, pair % per
            corrs.append(total[r, stage, at * BW:(at + 1) * BW, :] / size)
        turned = [corr.T for corr in corrs]
        squares = []
        for corr, corr_t in zip(corrs, turned):
            squares += [product(corr, corr_t), product(corr_t, corr)]
        roots = inverse_roots(squares, eye)
        results = []
        for at in range(pairs):
            one, two = roots[2 * at], roots[2 * at + 1]
            upper = jnp.concatenate([one, -sign * product(corrs[at], two)], axis=1)
            lower = jnp.concatenate([sign * product(turned[at], one), two], axis=1)
            results.append(jnp.concatenate([upper, lower], axis=0))
        return results

    def apply(r, pair, rotation):
        block = jnp.concatenate([buf[r, 2 * pair], buf[r, 2 * pair + 1]], axis=1)
        high, low = split(block)
        turn_high, turn_low = split(rotation)
        return dot(high, turn_high) + dot(low, turn_high) + dot(high, turn_low)

    def swap(r):
        return pltpu.make_async_remote_copy(
            src_ref=spare.at[r],
            dst_ref=buf.at[r + 1, slots - 1],
            send_sem=swap_send.at[r],
            recv_sem=swap_recv.at[r],
            device_id={"col": 1 - col},
            device_id_type=MESH,
        )

    def place(r, pair, result):
        first, second = result[:, :BW], result[:, BW:]
        if pair == pairs - 1:
            spare[r] = first
            swap(r).start()
        else:
            buf[r + 1, 2 * pair + 2 if pair else 0] = first
        buf[r + 1, 2 * pair - 1 if pair else 2] = second

    def turn_slots(rotation):
        swapped = jnp.concatenate([rotation[:, BW:], rotation[:, :BW]], axis=1)
        return jnp.where(col == 0, rotation, swapped)

    def launch(r, pair):
        if r == 0:
            loads[2 * pair].wait()
            loads[2 * pair + 1].wait()
        elif pair == pairs - 1:
            swap(r - 1).wait_recv()
        gram(r, pair)
        if pair % per == 0:
            if r == 0 and pair // per == stages - 1:
                pl.semaphore_wait(barrier, n)
            send_parts(r, pair // per)

    def rotate_round(r, last):
        turns = rotations(r, traces_of(r), identity())
        for pair in reversed(range(pairs)):
            turn = turns[pair]
            if last:
                result = apply(r, pair, turn)
                for side in range(2):
                    buf[r + 1, 2 * pair + side] = result[:, side * BW:(side + 1) * BW]
                    store(2 * pair + side).start()
            else:
                if pair == 0:
                    turn = turn_slots(turn)
                place(r, pair, apply(r, pair, turn))
                if pair < pairs - 1:
                    launch(r + 1, pair + 1)
                if pair == 0:
                    launch(r + 1, 0)

    def store(slot):
        return pltpu.make_async_copy(
            buf.at[ROUNDS, slot], out_ref.at[:, columns(slot)], out_sem.at[slot]
        )

    for pair in reversed(range(pairs)):
        launch(0, pair)
    for r in range(ROUNDS):
        send_traces(r)
        for stage in reversed(range(stages)):
            send_sums(r, stage)
        rotate_round(r, r == ROUNDS - 1)

    for slot in range(slots):
        store(slot).wait()
    for r in range(ROUNDS):
        if r < ROUNDS - 1:
            swap(r).wait_send()
        held = norms.at[r, pl.ds(0, n - 1)]
        pltpu.make_async_copy(held, held, norm_send.at[r]).wait()
        for stage in range(stages):
            everyone = landed.at[r, stage]
            pltpu.make_async_copy(everyone, everyone, rs_send.at[r, stage]).wait()
            held = gathered_bytes(r, stage)
            pltpu.make_async_copy(held, held, ag_send.at[r, stage]).wait()


def shards(n, patches):
    rows, width = patches.shape
    pairs = width // (2 * BW)
    per = max(1, min(pairs, 8 * n // BW))
    stages = pairs // per
    chunk = per * BW // n
    return pl.pallas_call(
        functools.partial(kernel, n, pairs, per),
        out_shape=jax.ShapeDtypeStruct((rows, width), F32),
        in_specs=[pl.BlockSpec(memory_space=pl.ANY)],
        out_specs=pl.BlockSpec(memory_space=pl.ANY),
        scratch_shapes=[
            pltpu.VMEM((ROUNDS + 1, 2 * pairs, rows, BW), F32),
            pltpu.VMEM((ROUNDS, stages, per * BW, BW), F32),
            pltpu.VMEM((ROUNDS, stages, n - 1, chunk, BW), F32),
            pltpu.VMEM((ROUNDS, stages, per * BW, BW), F32),
            pltpu.VMEM((ROUNDS - 1, rows, BW), F32),
            pltpu.VMEM((ROUNDS, n, 2 * pairs, BW), F32),
            pltpu.SemaphoreType.DMA((2 * pairs,)),
            pltpu.SemaphoreType.DMA((2 * pairs,)),
            pltpu.SemaphoreType.DMA((ROUNDS,)),
            pltpu.SemaphoreType.DMA((ROUNDS,)),
            pltpu.SemaphoreType.DMA((ROUNDS, stages)),
            pltpu.SemaphoreType.DMA((ROUNDS, stages)),
            pltpu.SemaphoreType.DMA((ROUNDS, stages)),
            pltpu.SemaphoreType.DMA((ROUNDS, stages)),
            pltpu.SemaphoreType.DMA((ROUNDS - 1,)),
            pltpu.SemaphoreType.DMA((ROUNDS - 1,)),
        ],
        compiler_params=pltpu.CompilerParams(
            collective_id=0, has_side_effects=True, vmem_limit_bytes=60 * 1024 * 1024
        ),
    )(patches)


def solution(mesh):
    placed = P(("groups", "row"), "col")
    return jax.shard_map(
        functools.partial(shards, mesh.shape["row"]),
        mesh=mesh,
        in_specs=(placed,),
        out_specs=placed,
        check_vma=False,
    )
```

```python
import functools

import jax
import jax.numpy as jnp
from jax import lax
from jax.experimental import pallas as pl
from jax.experimental.pallas import tpu as pltpu
from jax.sharding import PartitionSpec as P

BW = 128
ROUNDS = 4
STEPS = 8
EXACT = 3
MESH = pl.DeviceIdType.MESH
F32 = jnp.float32
BF16 = jnp.bfloat16


def split(x):
    high = x.astype(BF16)
    return high, (x - high.astype(F32)).astype(BF16)


def dot(a, b):
    return jnp.dot(a, b, preferred_element_type=F32)


def product(a, b):
    width = b.shape[1]
    right = jnp.concatenate(split(b), axis=1)
    both = dot(jnp.concatenate(split(a), axis=1), jnp.concatenate([right, right], axis=0))
    return both[:, :width] + both[:, width:]


def rough(a, b):
    return dot(a.astype(BF16), b.astype(BF16))


def identity():
    rows = lax.broadcasted_iota(jnp.int32, (BW, BW), 0)
    columns = lax.broadcasted_iota(jnp.int32, (BW, BW), 1)
    return jnp.where(rows == columns, 1.0, 0.0).astype(F32)


def inverse_roots(squares, eye):
    errors = [0.5 * eye - 0.5 * square for square in squares]
    roots = [eye + 0.5 * error for error in errors]
    for step in range(1, STEPS):
        times = product if step < EXACT else rough
        if step <= EXACT:
            seconds = [times(error, error) for error in errors]
        else:
            both = [rough(error, jnp.concatenate([error, root], axis=1))
                    for error, root in zip(errors, roots)]
            seconds = [two[:, :BW] for two in both]
            roots = [root + 0.5 * two[:, BW:] for root, two in zip(roots, both)]
        thirds = [times(second, error) for second, error in zip(seconds, errors)]
        errors = [0.75 * second + 0.25 * third for second, third in zip(seconds, thirds)]
        if step < EXACT:
            roots = [root + 0.5 * times(root, error) for root, error in zip(roots, errors)]
    roots = [root + 0.5 * rough(error, root) for root, error in zip(roots, errors)]
    return [root * 0.7071067811865476 for root in roots]


def kernel(n, pairs, per, x_ref, out_ref, buf, part, landed, half, crossed, total, spare, norms,
           in_sem, out_sem, norm_send, norm_recv, rs_send, rs_recv, cross_send, cross_recv, ag_send, ag_recv, swap_send, swap_recv):
    me = lax.axis_index("row")
    col = lax.axis_index("col")
    stages = pairs // per
    slots = 2 * pairs
    m = n // 2
    chunk = per * BW // m
    inner = lax.rem(me, m)
    near_at = [lax.rem(inner + j, m) for j in range(m)]
    near = [me - inner + at for at in near_at]
    far = lax.rem(me + m, n)
    own = [lax.rem(me + j, n) for j in range(n)]
    order = sorted(range(1, n), key=lambda j: abs(2 * j - n))
    sign = jnp.where(col == 0, 1.0, -1.0).astype(F32)

    def columns(slot):
        place = jnp.where(col == 0, slot, slots - 1 - slot)
        return pl.ds(pl.multiple_of(place * BW, BW), BW)

    loads = [
        pltpu.make_async_copy(x_ref.at[:, columns(slot)], buf.at[0, slot], in_sem.at[slot])
        for slot in range(slots)
    ]
    for load in reversed(loads):
        load.start()

    barrier = pltpu.get_barrier_semaphore()
    for j in range(1, n):
        pl.semaphore_signal(barrier, inc=1, device_id={"row": own[j]}, device_id_type=MESH)
    pl.semaphore_signal(barrier, inc=1, device_id={"col": 1 - col}, device_id_type=MESH)

    def gram(r, pair):
        stage, at = pair // per, pair % per
        left_halves = jnp.concatenate(split(buf[r, 2 * pair]), axis=1)
        right_halves = jnp.concatenate(split(buf[r, 2 * pair + 1]), axis=1)
        both = lax.dot_general(
            left_halves, right_halves, (((0,), (0,)), ((), ())), preferred_element_type=F32
        )
        cross = both[:BW, :BW] + both[:BW, BW:] + both[BW:, :BW] + both[BW:, BW:]
        part[r, stage, at * BW:(at + 1) * BW, :] = cross

    def send_traces(r):
        blocks = [buf[r, slot] for slot in range(slots)]
        sums = [jnp.sum(block * block, axis=0, keepdims=True) for block in blocks]
        norms[r, n - 1] = jnp.concatenate(sums, axis=0)
        for j in order:
            pltpu.make_async_remote_copy(
                src_ref=norms.at[r, n - 1],
                dst_ref=norms.at[r, j - 1],
                send_sem=norm_send.at[r],
                recv_sem=norm_recv.at[r],
                device_id={"row": own[j]},
                device_id_type=MESH,
            ).start()

    def traces_of(r):
        held = norms.at[r, pl.ds(0, n - 1)]
        pltpu.make_async_copy(held, held, norm_recv.at[r]).wait()
        summed = norms[r, 0]
        for j in range(1, n):
            summed = summed + norms[r, j]
        return jnp.sum(summed, axis=1, keepdims=True)

    def send_parts(r, stage):
        for j in range(1, m):
            rows = pl.ds(pl.multiple_of(near_at[j] * chunk, 8), chunk)
            pltpu.make_async_remote_copy(
                src_ref=part.at[r, stage, rows],
                dst_ref=landed.at[r, stage, j - 1],
                send_sem=rs_send.at[r, stage],
                recv_sem=rs_recv.at[r, stage],
                device_id={"row": near[j]},
                device_id_type=MESH,
            ).start()

    def cross(r, stage):
        return pltpu.make_async_remote_copy(
            src_ref=half.at[r, stage],
            dst_ref=crossed.at[r, stage],
            send_sem=cross_send.at[r, stage],
            recv_sem=cross_recv.at[r, stage],
            device_id={"row": far},
            device_id_type=MESH,
        )

    def send_half(r, stage):
        everyone = landed.at[r, stage]
        pltpu.make_async_copy(everyone, everyone, rs_recv.at[r, stage]).wait()
        summed = part[r, stage, pl.ds(pl.multiple_of(inner * chunk, 8), chunk)]
        for j in range(m - 1):
            summed = summed + landed[r, stage, j]
        half[r, stage] = summed
        cross(r, stage).start()

    def send_sums(r, stage):
        cross(r, stage).wait_recv()
        mine = total.at[r, stage, pl.ds(pl.multiple_of(inner * chunk, 8), chunk)]
        mine[...] = half[r, stage] + crossed[r, stage]
        for j in range(1, m):
            pltpu.make_async_remote_copy(
                src_ref=mine,
                dst_ref=mine,
                send_sem=ag_send.at[r, stage],
                recv_sem=ag_recv.at[r, stage],
                device_id={"row": near[j]},
                device_id_type=MESH,
            ).start()

    def gathered_bytes(r, stage):
        return total.at[r, stage, pl.ds(0, (m - 1) * chunk)]

    def rotations(r, traces, eye):
        for stage in reversed(range(stages)):
            held = gathered_bytes(r, stage)
            pltpu.make_async_copy(held, held, ag_recv.at[r, stage]).wait()
        corrs = []
        for pair in range(pairs):
            size = jnp.sqrt(traces[2 * pair:2 * pair + 1] * traces[2 * pair + 1:2 * pair + 2])
            stage, at = pair // per, pair % per
            corrs.append(total[r, stage, at * BW:(at + 1) * BW, :] / size)
        turned = [corr.T for corr in corrs]
        squares = []
        for corr, corr_t in zip(corrs, turned):
            squares += [product(corr, corr_t), product(corr_t, corr)]
        roots = inverse_roots(squares, eye)
        results = []
        for at in range(pairs):
            one, two = roots[2 * at], roots[2 * at + 1]
            upper = jnp.concatenate([one, -sign * product(corrs[at], two)], axis=1)
            lower = jnp.concatenate([sign * product(turned[at], one), two], axis=1)
            results.append(jnp.concatenate([upper, lower], axis=0))
        return results

    def apply(r, pair, rotation):
        block = jnp.concatenate([buf[r, 2 * pair], buf[r, 2 * pair + 1]], axis=1)
        high, low = split(block)
        turn_high, turn_low = split(rotation)
        return dot(high, turn_high) + dot(low, turn_high) + dot(high, turn_low)

    def swap(r):
        return pltpu.make_async_remote_copy(
            src_ref=spare.at[r],
            dst_ref=buf.at[r + 1, slots - 1],
            send_sem=swap_send.at[r],
            recv_sem=swap_recv.at[r],
            device_id={"col": 1 - col},
            device_id_type=MESH,
        )

    def place(r, pair, result):
        first, second = result[:, :BW], result[:, BW:]
        if pair == pairs - 1:
            spare[r] = first
            swap(r).start()
        else:
            buf[r + 1, 2 * pair + 2 if pair else 0] = first
        buf[r + 1, 2 * pair - 1 if pair else 2] = second

    def turn_slots(rotation):
        swapped = jnp.concatenate([rotation[:, BW:], rotation[:, :BW]], axis=1)
        return jnp.where(col == 0, rotation, swapped)

    def launch(r, pair):
        if r == 0:
            loads[2 * pair].wait()
            loads[2 * pair + 1].wait()
        elif pair == pairs - 1:
            swap(r - 1).wait_recv()
        gram(r, pair)
        if pair % per == 0:
            if r == 0 and pair // per == stages - 1:
                pl.semaphore_wait(barrier, n)
            send_parts(r, pair // per)

    def rotate_round(r, last):
        turns = rotations(r, traces_of(r), identity())
        for pair in reversed(range(pairs)):
            turn = turns[pair]
            if last:
                result = apply(r, pair, turn)
                for side in range(2):
                    buf[r + 1, 2 * pair + side] = result[:, side * BW:(side + 1) * BW]
                    store(2 * pair + side).start()
            else:
                if pair == 0:
                    turn = turn_slots(turn)
                place(r, pair, apply(r, pair, turn))
                if pair < pairs - 1:
                    launch(r + 1, pair + 1)
                if pair == 0:
                    launch(r + 1, 0)

    def store(slot):
        return pltpu.make_async_copy(
            buf.at[ROUNDS, slot], out_ref.at[:, columns(slot)], out_sem.at[slot]
        )

    for pair in reversed(range(pairs)):
        launch(0, pair)
    for r in range(ROUNDS):
        send_traces(r)
        for stage in reversed(range(stages)):
            send_half(r, stage)
        for stage in reversed(range(stages)):
            send_sums(r, stage)
        rotate_round(r, r == ROUNDS - 1)

    for slot in range(slots):
        store(slot).wait()
    for r in range(ROUNDS):
        if r < ROUNDS - 1:
            swap(r).wait_send()
        held = norms.at[r, pl.ds(0, n - 1)]
        pltpu.make_async_copy(held, held, norm_send.at[r]).wait()
        for stage in range(stages):
            everyone = landed.at[r, stage]
            pltpu.make_async_copy(everyone, everyone, rs_send.at[r, stage]).wait()
            cross(r, stage).wait_send()
            held = gathered_bytes(r, stage)
            pltpu.make_async_copy(held, held, ag_send.at[r, stage]).wait()


def shards(n, patches):
    rows, width = patches.shape
    pairs = width // (2 * BW)
    m = n // 2
    per = max(1, min(pairs, 8 * m // BW))
    stages = pairs // per
    chunk = per * BW // m
    return pl.pallas_call(
        functools.partial(kernel, n, pairs, per),
        out_shape=jax.ShapeDtypeStruct((rows, width), F32),
        in_specs=[pl.BlockSpec(memory_space=pl.ANY)],
        out_specs=pl.BlockSpec(memory_space=pl.ANY),
        scratch_shapes=[
            pltpu.VMEM((ROUNDS + 1, 2 * pairs, rows, BW), F32),
            pltpu.VMEM((ROUNDS, stages, per * BW, BW), F32),
            pltpu.VMEM((ROUNDS, stages, m - 1, chunk, BW), F32),
            pltpu.VMEM((ROUNDS, stages, chunk, BW), F32),
            pltpu.VMEM((ROUNDS, stages, chunk, BW), F32),
            pltpu.VMEM((ROUNDS, stages, per * BW, BW), F32),
            pltpu.VMEM((ROUNDS - 1, rows, BW), F32),
            pltpu.VMEM((ROUNDS, n, 2 * pairs, BW), F32),
            pltpu.SemaphoreType.DMA((2 * pairs,)),
            pltpu.SemaphoreType.DMA((2 * pairs,)),
            pltpu.SemaphoreType.DMA((ROUNDS,)),
            pltpu.SemaphoreType.DMA((ROUNDS,)),
            pltpu.SemaphoreType.DMA((ROUNDS, stages)),
            pltpu.SemaphoreType.DMA((ROUNDS, stages)),
            pltpu.SemaphoreType.DMA((ROUNDS, stages)),
            pltpu.SemaphoreType.DMA((ROUNDS, stages)),
            pltpu.SemaphoreType.DMA((ROUNDS, stages)),
            pltpu.SemaphoreType.DMA((ROUNDS, stages)),
            pltpu.SemaphoreType.DMA((ROUNDS - 1,)),
            pltpu.SemaphoreType.DMA((ROUNDS - 1,)),
        ],
        compiler_params=pltpu.CompilerParams(
            collective_id=0, has_side_effects=True, vmem_limit_bytes=60 * 1024 * 1024
        ),
    )(patches)


def solution(mesh):
    placed = P(("groups", "row"), "col")
    return jax.shard_map(
        functools.partial(shards, mesh.shape["row"]),
        mesh=mesh,
        in_specs=(placed,),
        out_specs=placed,
        check_vma=False,
    )
```
